256 devices in a mesh: seq: 16 (over z, core), fft: 16 (over y, x).
Axes of the slice: x: 4, y: 4, z: 8, core: 2. Of those that a mesh axis runs over, the one named last changes fastest.
Arguments:
- projections: bfloat16 [3, 8192, 4096], P(None, 'seq', 'fft'), may hold values from -6 to 6
- taps: float32 [7, 3, 4096], P(None, None, 'fft'), may hold values from -2 to 2
- rates: float32 [4096, 16], replicated, may hold values from 6.1035156e-05 to 0.03
- residues: float32 [4096, 16], replicated, may hold values from -1 to 1
- skip: float32 [4096], P('fft'), may hold values from -2 to 2
Outputs:
- mixed: bfloat16 [8192, 4096], P('seq', 'fft')
The draws below stay inside these ranges and needn't reach their ends.
All inputs are finite; a program needn't handle non-finite values.
Results may differ from the reference program's by a relative error of at most 0.007.
Values may be sent and summed in bfloat16 or wider, within the bound.
No kernel may reach another device: no remote copies, remote signals or barrier semaphores. Data moves between devices by JAX's collectives and lax.ppermute only.
A program may use at most 128 MiB of HBM per device.

```python
import math
import jax
import jax.numpy as jnp
from jax import lax

D = 4096
KS = 7
MODES = 16
SEQ_LEN = 8192


def block_scale(rng, dims, shards, smallest, top_value):
    loudness, own = 1.0, jax.random.fold_in(rng, 6)
    for dim, shards_of in shards:
        draws = jnp.exp(jax.random.uniform(jax.random.fold_in(own, dim), (shards_of,), jnp.float32, smallest / len(shards), top_value / len(shards)))
        loudness = loudness * jnp.repeat(draws, dims[dim] // shards_of).reshape([-1 if axis == dim else 1 for axis in range(len(dims))])
    return loudness


def centred(key, dims, spread, reach, split=(), dtype=jnp.bfloat16):
    array = jax.random.normal(key, dims, jnp.float32) * spread
    if len(split) > 0:
        array = block_scale(key, dims, split, -0.22, 0.18) * array
    return jnp.clip(array, min=-reach, max=reach).astype(dtype)


def setup_inputs(seed: int = 0) -> dict:
    seeds = jax.random.split(jax.random.key(seed), 6)
    return {
        "projections": centred(seeds[0], (3, SEQ_LEN, D), 1.0, 6.0, ((1, 16), (2, 16))),
        "taps": centred(seeds[1], (KS, 3, D), KS ** -0.5, 2.0, ((2, 16),), jnp.float32),
        "rates": jnp.clip(jnp.exp(jax.random.uniform(seeds[2], (D, MODES), jnp.float32, math.log(6.103515625e-05), math.log(0.03))), 6.103515625e-05, 0.03),
        "residues": centred(seeds[3], (D, MODES), 0.25, 1.0, (), jnp.float32),
        "skip": centred(seeds[4], (D,), 0.5, 2.0, ((0, 16),), jnp.float32),
    }


def causal_filter(projections, taps):
    values = projections.astype(jnp.float32)
    tap_count = taps.shape[0]
    tok_count = values.shape[1]
    padded = jnp.pad(values, ((0, 0), (tap_count - 1, 0), (0, 0)))
    filtered = jnp.zeros(values.shape, jnp.float32)
    for offset in range(tap_count):
        begin_row = tap_count - 1 - offset
        filtered = filtered + taps[offset][:, None, :] * padded[:, begin_row:begin_row + tok_count, :]
    return filtered

def block_convolve(operands):
    inputs_block, rates_block, residues_block = operands
    seq_count = inputs_block.shape[0]
    positions = jnp.arange(seq_count).astype(jnp.float32)[:, None]
    kernel = jnp.zeros(inputs_block.shape, jnp.float32)
    for mode_index in range(rates_block.shape[1]):
        rate_now = rates_block[:, mode_index]
        scale_now = residues_block[:, mode_index] * jnp.sqrt(-jnp.expm1(-2.0 * rate_now))
        kernel = kernel + scale_now[None, :] * jnp.exp(-rate_now[None, :] * positions)
    full_len = 2 * seq_count
    product = jnp.fft.rfft(inputs_block, n=full_len, axis=0) * jnp.fft.rfft(kernel, n=full_len, axis=0)
    return jnp.fft.irfft(product, n=full_len, axis=0)[:seq_count]

def reference(projections, taps, rates, residues, skip):
    filtered = causal_filter(projections, taps)
    gated_input = (filtered[1] * filtered[2]).astype(jnp.bfloat16)
    seq_count, channels = gated_input.shape
    block_width = 128
    block_count = channels // block_width
    blocks = gated_input.astype(jnp.float32).reshape(seq_count, block_count, block_width).transpose(1, 0, 2)
    rate_blocks = rates.reshape(block_count, block_width, rates.shape[1])
    residue_blocks = residues.reshape(block_count, block_width, residues.shape[1])
    convolved = lax.map(block_convolve, (blocks, rate_blocks, residue_blocks))
    long_out = convolved.transpose(1, 0, 2).reshape(seq_count, channels).astype(jnp.bfloat16)
    mixed = filtered[0] * (long_out.astype(jnp.float32) + skip[None, :] * gated_input.astype(jnp.float32))
    return mixed.astype(jnp.bfloat16)
```

```python
import jax
import jax.numpy as jnp
from jax import lax
from jax.experimental import pallas as pl
from jax.experimental.pallas import tpu as pltpu
from jax.sharding import PartitionSpec as P

CHUNKS = 8
LANES = 128
PAD = 8


def rounded(values):
    return values.astype(jnp.bfloat16).astype(jnp.float32)


def spread(row):
    return jnp.broadcast_to(row, (CHUNKS, row.shape[-1]))


def pairwise_sum(terms):
    while len(terms) > 1:
        joined = [a + b for a, b in zip(terms[0::2], terms[1::2])]
        terms = joined + ([terms[-1]] if len(terms) % 2 else [])
    return terms[0]


def one_minus_exp(y):
    series = jnp.ones_like(y)
    for divisor in (7.0, 6.0, 5.0, 4.0, 3.0, 2.0):
        series = 1.0 - y * (1.0 / divisor) * series
    return jnp.where(y < 0.1, y * series, 1.0 - jnp.exp(-y))


def chunk_rows(buffer, first, count, stride):
    return [buffer[pl.ds(PAD + first + k, CHUNKS, stride=stride), :] for k in range(count)]


def filter_chunks(buffer, taps, length, emit):
    tap_count = len(taps)
    step = 8
    for first in range(0, length, step):
        rows = chunk_rows(buffer, first - (tap_count - 1), step + tap_count - 1, length)
        for k in range(step):
            terms = [taps[i] * rows[k + tap_count - 1 - i] for i in range(tap_count)]
            emit(first + k, pairwise_sum(terms))


def state_kernel(
    rates_hbm, residues_hbm, taps_ref, tokens_hbm, gated_ref, ends_ref, state_ref, head_ref, tail_ref, rates_ref, scale_ref,
    bits_ref, head_bits_ref, tail_bits_ref, residues_ref, one_ref, two_ref, sems,
):
    channels = rates_ref.shape[1]
    mode_count = rates_ref.shape[0]
    token_count = bits_ref.shape[2]
    length = token_count // CHUNKS
    tap_count = taps_ref.shape[1]
    halo_rows = tap_count - 1
    halves = channels // LANES
    edge_rows = head_bits_ref.shape[0]
    start = pl.multiple_of(lax.axis_index("fft") * channels, channels)
    loads = []
    for half in range(halves):
        for q in (1, 2):
            copy = pltpu.make_async_copy(
                tokens_hbm.at[q, :, pl.ds(half * LANES, LANES)], bits_ref.at[half, q - 1], sems.at[2 * half + q - 1]
            )
            copy.start()
            loads.append(copy)
    late = [
        pltpu.make_async_copy(rates_hbm.at[:, pl.ds(start, channels)], rates_ref, sems.at[2 * halves]),
        pltpu.make_async_copy(residues_hbm.at[:, pl.ds(start, channels)], residues_ref, sems.at[2 * halves + 1]),
        pltpu.make_async_copy(tokens_hbm.at[0, 0:edge_rows, :], head_bits_ref, sems.at[2 * halves + 2]),
        pltpu.make_async_copy(
            tokens_hbm.at[0, token_count - edge_rows : token_count, :], tail_bits_ref, sems.at[2 * halves + 3]
        ),
    ]
    for copy in late:
        copy.start()
    sublane = lax.broadcasted_iota(jnp.int32, (CHUNKS, LANES), 0)
    keep = jnp.where(sublane == 0, jnp.where(lax.axis_index("seq") == 0, 1.0, 0.0), 1.0)
    to_end = -((CHUNKS - 1 - sublane) * length).astype(jnp.float32)
    zero_rows = jnp.zeros((PAD, LANES), jnp.float32)
    for half in range(halves):
        lanes = slice(half * LANES, (half + 1) * LANES)
        for buffer, q in ((one_ref, 1), (two_ref, 2)):
            loads[2 * half + q - 1].wait()
            buffer[half, 0:PAD, :] = zero_rows
            buffer[half, PAD:, :] = bits_ref[half, q - 1].astype(jnp.float32)
            head_ref[q, :, lanes] = buffer[half, PAD : 2 * PAD, :]
            tail_ref[q, :, lanes] = buffer[half, token_count:, :]

        def emit_one(j, row):
            gated_ref[j, :, lanes] = row

        def emit_gate(j, row):
            gated = rounded(gated_ref[j, :, lanes] * row)
            if j < halo_rows:
                gated = gated * keep
            gated_ref[j, :, lanes] = gated

        filter_chunks(one_ref.at[half], [spread(taps_ref[1, i : i + 1, lanes]) for i in range(tap_count)], length, emit_one)
        filter_chunks(two_ref.at[half], [spread(taps_ref[2, i : i + 1, lanes]) for i in range(tap_count)], length, emit_gate)
        if half == 0:
            for copy in late:
                copy.wait()
            head_ref[0] = head_bits_ref[...].astype(jnp.float32)[:PAD]
            tail_ref[0] = tail_bits_ref[...].astype(jnp.float32)[edge_rows - PAD :]
            scale_ref[...] = residues_ref[...] * jnp.sqrt(one_minus_exp(2.0 * rates_ref[...]))
        rates = rates_ref[:, lanes]
        decay = jnp.exp(-rates)
        decays = [spread(decay[m : m + 1]) for m in range(mode_count)]
        states = [gated_ref[0, :, lanes]] * mode_count
        for j in range(1, length):
            row = gated_ref[j, :, lanes]
            states = [d * h + row for d, h in zip(decays, states)]
        for m in range(mode_count):
            ends_ref[m, :, lanes] = states[m]
            weight = jnp.exp(spread(rates[m : m + 1]) * to_end)
            state_ref[m : m + 1, lanes] = jnp.sum(weight * states[m], axis=0, keepdims=True)


def local_kernel(
    rates_ref, scale_ref, taps_ref, skip_ref, zeroth_ref, gated_ref, local_ref, gate_ref, skip_row_ref, buffer_ref
):
    length = zeroth_ref.shape[1] // CHUNKS
    mode_count = rates_ref.shape[0]
    tap_count = taps_ref.shape[1]
    skip_row_ref[...] = skip_ref[...]
    buffer_ref[0:PAD, :] = jnp.zeros((PAD, LANES), jnp.float32)
    buffer_ref[PAD:, :] = zeroth_ref[0].astype(jnp.float32)

    def emit(j, row):
        gate_ref[j] = row

    filter_chunks(buffer_ref, [spread(taps_ref[0, i : i + 1, :]) for i in range(tap_count)], length, emit)
    decay = jnp.exp(-rates_ref[...])
    decays = [spread(decay[m : m + 1]) for m in range(mode_count)]
    scales = [spread(scale_ref[m : m + 1, :]) for m in range(mode_count)]
    states = [gated_ref[0]] * mode_count
    for j in range(length):
        if j > 0:
            row = gated_ref[j]
            states = [d * h + row for d, h in zip(decays, states)]
        local_ref[j] = pairwise_sum([c * h for c, h in zip(scales, states)])


def final_kernel(
    rates_ref, scale_ref, taps_ref, skip_ref, incoming_ref, halo_ref, head_ref, ends_ref, gated_ref, local_ref,
    gate_ref, out_ref, edge_ref, rows_ref,
):
    length = gated_ref.shape[0]
    mode_count = rates_ref.shape[0]
    tap_count = taps_ref.shape[1]
    halo_rows = tap_count - 1
    sublane = lax.broadcasted_iota(jnp.int32, (CHUNKS, LANES), 0)
    edges = []
    for q in range(3):
        edge_ref[q, 0:PAD, :] = halo_ref[q]
        edge_ref[q, PAD : 2 * PAD, :] = head_ref[q, 0:PAD, :]
        edges.append(
            pairwise_sum([taps_ref[q, i : i + 1, :] * edge_ref[q, PAD - i : 2 * PAD - i, :] for i in range(tap_count)])
        )
    edge_gated = rounded(edges[1] * edges[2]) * jnp.where(lax.axis_index("seq") == 0, 0.0, 1.0)
    rates = rates_ref[...]
    scale = scale_ref[...]
    decay = jnp.exp(-rates)
    edge_state = jnp.zeros_like(decay)
    for t in range(halo_rows):
        edge_state = decay * edge_state + edge_gated[t : t + 1]
    edge_state = edge_state * jnp.exp(-rates * float(length - halo_rows))
    chunk_decay = jnp.exp(-rates * float(length))
    decays = [spread(decay[m : m + 1]) for m in range(mode_count)]
    states = []
    for m in range(mode_count):
        factor = spread(chunk_decay[m : m + 1])
        ends = ends_ref[m] + jnp.where(sublane == 0, spread(edge_state[m : m + 1]), 0.0)
        carried = jnp.where(sublane == 0, spread(incoming_ref[m : m + 1, :]), pltpu.roll(ends, 1, 0))
        for distance in (1, 2, 4):
            carried = carried + jnp.where(sublane >= distance, factor * pltpu.roll(carried, distance, 0), 0.0)
            factor = factor * factor
        states.append(carried * spread(scale[m : m + 1]))
    skip = spread(skip_ref[...])
    for j in range(length):
        states = [d * h for d, h in zip(decays, states)]
        gated, gate = gated_ref[j], gate_ref[j]
        if j < halo_rows:
            new = jnp.where(sublane == 0, spread(edge_gated[j : j + 1]), 0.0)
            states = [h + spread(scale[m : m + 1]) * new for m, h in enumerate(states)]
            gated = gated + new
            gate = jnp.where(sublane == 0, spread(edges[0][j : j + 1]), gate)
        long_out = rounded(local_ref[j] + pairwise_sum(states))
        rows_ref[pl.ds(j, CHUNKS, stride=length), :] = gate * (long_out + skip * gated)
    out_ref[...] = rows_ref[...].astype(jnp.bfloat16)


def by_lanes(*dims):
    return pl.BlockSpec((*dims, LANES), lambda i: (*(0 for _ in dims), i))


def one_projection(q, tokens):
    return pl.BlockSpec((1, tokens, LANES), lambda i: (q, 0, i))


def shape32(*dims):
    return jax.ShapeDtypeStruct(dims, jnp.float32)


PARAMS = pltpu.CompilerParams(vmem_limit_bytes=24 * 1024 * 1024)


def on_device(projections, taps, rates, residues, skip):
    tap_count = taps.shape[0]
    halo_rows = tap_count - 1
    _, tokens, channels = projections.shape
    mode_count = rates.shape[1]
    length = tokens // CHUNKS
    grid = (channels // LANES,)
    halves = channels // LANES
    count = lax.axis_size("seq")
    index = lax.axis_index("seq")
    taps = taps.transpose(1, 0, 2)
    hbm = pl.BlockSpec(memory_space=pltpu.HBM)
    vmem = pl.BlockSpec(memory_space=pltpu.VMEM)
    gated, ends, state, head, tail, rates_own, scale = pl.pallas_call(
        state_kernel,
        out_shape=(
            shape32(length, CHUNKS, channels),
            shape32(mode_count, CHUNKS, channels),
            shape32(mode_count, channels),
            shape32(3, PAD, channels),
            shape32(3, PAD, channels),
            shape32(mode_count, channels),
            shape32(mode_count, channels),
        ),
        in_specs=[hbm, hbm, vmem, hbm],
        out_specs=(vmem,) * 7,
        scratch_shapes=[
            pltpu.VMEM((halves, 2, tokens, LANES), jnp.bfloat16),
            pltpu.VMEM((2 * PAD, channels), jnp.bfloat16),
            pltpu.VMEM((2 * PAD, channels), jnp.bfloat16),
            pltpu.VMEM((mode_count, channels), jnp.float32),
            pltpu.VMEM((halves, PAD + tokens, LANES), jnp.float32),
            pltpu.VMEM((halves, PAD + tokens, LANES), jnp.float32),
            pltpu.SemaphoreType.DMA((2 * halves + 4,)),
        ],
        compiler_params=PARAMS,
        name="state",
    )(*(pltpu.with_memory_space_constraint(array, pltpu.HBM) for array in (rates.T, residues.T)), taps,
      pltpu.with_memory_space_constraint(projections, pltpu.HBM))
    taps_spec = by_lanes(3, tap_count)
    modes_spec = by_lanes(mode_count)
    grid_spec = by_lanes(length, CHUNKS)
    ends_spec = by_lanes(mode_count, CHUNKS)
    local, gate, skip_row = pl.pallas_call(
        local_kernel,
        out_shape=(shape32(length, CHUNKS, channels),) * 2 + (shape32(1, channels),),
        grid=grid,
        in_specs=[modes_spec, modes_spec, taps_spec, by_lanes(1), one_projection(0, tokens), grid_spec],
        out_specs=(grid_spec, grid_spec, by_lanes(1)),
        scratch_shapes=[pltpu.VMEM((PAD + tokens, LANES), jnp.float32)],
        compiler_params=PARAMS,
        name="local",
    )(rates_own, scale, taps, skip[None, :], projections, gated)

    def decayed(steps):
        return jnp.exp(-rates_own * jnp.asarray(steps, jnp.float32))

    def exchange(state, first, last, flip):
        high = lax.reduce_precision(state, 8, 7)
        rows = [high, state - high, last.reshape(3 * PAD, channels), first.reshape(2 * PAD, channels)]
        packed = jnp.concatenate(rows, axis=0).astype(jnp.bfloat16)
        packed = lax.ppermute(packed, "seq", [(i, i ^ flip) for i in range(count)]).astype(jnp.float32)
        edges = packed[2 * mode_count :].reshape(5, PAD, channels)
        return packed[:mode_count] + packed[mode_count : 2 * mode_count], edges[3:], edges[:3]

    halo = jnp.zeros_like(tail)
    prefix = jnp.zeros_like(state)
    first, last = head[1:], tail
    size = 1
    while size < count:
        flip = {1: 1, 2: 3, 4: 5, 8: 13}.get(size, size)
        other_state, other_first, other_last = exchange(state, first, last, flip)
        is_right = index // size % 2 == 1
        left_last = jnp.where(is_right, other_last, last)
        right_first = jnp.where(is_right, first, other_first)
        left_state = jnp.where(is_right, other_state, state)
        right_state = jnp.where(is_right, state, other_state)
        joined = jnp.concatenate([left_last[1:], right_first], axis=1)
        edge = sum(taps[1:, i, None, :] * joined[:, PAD - i : 2 * PAD - i, :] for i in range(tap_count))
        gates = rounded(edge[0] * edge[1])
        edge_state = jnp.zeros_like(state)
        for t in range(halo_rows):
            edge_state = decayed(1.0) * edge_state + gates[t][None, :]
        offset = (index % size * tokens).astype(jnp.float32)
        is_first = index % size == 0
        arriving = decayed(offset) * left_state
        arriving = arriving + jnp.where(is_first, 0.0, decayed(jnp.maximum(offset - halo_rows, 0.0))) * edge_state
        prefix = jnp.where(is_right, prefix + arriving, prefix)
        halo = jnp.where(is_right & is_first, other_last, halo)
        block = float(size * tokens)
        state = right_state + decayed(block - halo_rows) * edge_state + decayed(block) * left_state
        first = jnp.where(is_right, other_first, first)
        last = jnp.where(is_right, last, other_last)
        size *= 2
        if size * 2 == count:
            state, local, gate = lax.optimization_barrier((state, local, gate))
    return pl.pallas_call(
        final_kernel,
        out_shape=jax.ShapeDtypeStruct((tokens, channels), jnp.bfloat16),
        grid=grid,
        in_specs=[
            modes_spec, modes_spec, taps_spec, by_lanes(1), modes_spec, by_lanes(3, PAD), by_lanes(3, PAD),
            ends_spec, grid_spec, grid_spec, grid_spec,
        ],
        out_specs=by_lanes(tokens),
        scratch_shapes=[
            pltpu.VMEM((3, 2 * PAD, LANES), jnp.float32),
            pltpu.VMEM((tokens, LANES), jnp.float32),
        ],
        compiler_params=PARAMS,
        name="final",
    )(rates_own, scale, taps, skip_row, prefix, halo, head, ends, gated, local, gate)


def solution(mesh):
    in_specs = (P(None, "seq", "fft"), P(None, None, "fft"), P(), P(), P("fft"))
    out_specs = P("seq", "fft")
    return jax.shard_map(on_device, mesh=mesh, in_specs=in_specs, out_specs=out_specs, check_vma=False)
```

```python
import jax
import jax.numpy as jnp
from jax import lax
from jax.experimental import pallas as pl
from jax.experimental.pallas import tpu as pltpu
from jax.sharding import PartitionSpec as P

CHUNKS = 8
LANES = 128
PAD = 8


def rounded(values):
    return values.astype(jnp.bfloat16).astype(jnp.float32)


def spread(row):
    return jnp.broadcast_to(row, (CHUNKS, row.shape[-1]))


def pairwise_sum(terms):
    while len(terms) > 1:
        joined = [a + b for a, b in zip(terms[0::2], terms[1::2])]
        terms = joined + ([terms[-1]] if len(terms) % 2 else [])
    return terms[0]


def one_minus_exp(y):
    series = jnp.ones_like(y)
    for divisor in (7.0, 6.0, 5.0, 4.0, 3.0, 2.0):
        series = 1.0 - y * (1.0 / divisor) * series
    return jnp.where(y < 0.1, y * series, 1.0 - jnp.exp(-y))


def chunk_rows(buffer, first, count, stride):
    return [buffer[pl.ds(PAD + first + k, CHUNKS, stride=stride), :] for k in range(count)]


def filter_chunks(buffer, taps, length, emit):
    tap_count = len(taps)
    step = 8
    for first in range(0, length, step):
        rows = chunk_rows(buffer, first - (tap_count - 1), step + tap_count - 1, length)
        for k in range(step):
            terms = [taps[i] * rows[k + tap_count - 1 - i] for i in range(tap_count)]
            emit(first + k, pairwise_sum(terms))


def state_kernel(
    rates_hbm, residues_hbm, taps_hbm, skip_hbm, tokens_hbm,
    gated_ref, ends_ref, state_ref, head_ref, tail_ref, rates_ref, scale_ref, taps_ref, skip_ref,
    bits_ref, head_bits_ref, tail_bits_ref, residues_ref, one_ref, two_ref, sems,
):
    channels = rates_ref.shape[1]
    mode_count = rates_ref.shape[0]
    token_count = bits_ref.shape[2]
    length = token_count // CHUNKS
    tap_count = taps_ref.shape[1]
    halo_rows = tap_count - 1
    halves = channels // LANES
    edge_rows = head_bits_ref.shape[0]
    start = pl.multiple_of(lax.axis_index("fft") * channels, channels)
    loads = []
    for half in range(halves):
        for q in (1, 2):
            copy = pltpu.make_async_copy(
                tokens_hbm.at[q, :, pl.ds(half * LANES, LANES)], bits_ref.at[half, q - 1], sems.at[2 * half + q - 1]
            )
            copy.start()
            loads.append(copy)
    early = [
        pltpu.make_async_copy(taps_hbm, taps_ref, sems.at[2 * halves + 4]),
        pltpu.make_async_copy(skip_hbm, skip_ref, sems.at[2 * halves + 5]),
    ]
    late = [
        pltpu.make_async_copy(rates_hbm.at[:, pl.ds(start, channels)], rates_ref, sems.at[2 * halves]),
        pltpu.make_async_copy(residues_hbm.at[:, pl.ds(start, channels)], residues_ref, sems.at[2 * halves + 1]),
        pltpu.make_async_copy(tokens_hbm.at[0, 0:edge_rows, :], head_bits_ref, sems.at[2 * halves + 2]),
        pltpu.make_async_copy(
            tokens_hbm.at[0, token_count - edge_rows : token_count, :], tail_bits_ref, sems.at[2 * halves + 3]
        ),
    ]
    for copy in early + late:
        copy.start()
    sublane = lax.broadcasted_iota(jnp.int32, (CHUNKS, LANES), 0)
    keep = jnp.where(sublane == 0, jnp.where(lax.axis_index("seq") == 0, 1.0, 0.0), 1.0)
    to_end = -((CHUNKS - 1 - sublane) * length).astype(jnp.float32)
    zero_rows = jnp.zeros((PAD, LANES), jnp.float32)
    for copy in early:
        copy.wait()
    for half in range(halves):
        lanes = slice(half * LANES, (half + 1) * LANES)
        for buffer, q in ((one_ref, 1), (two_ref, 2)):
            loads[2 * half + q - 1].wait()
            buffer[half, 0:PAD, :] = zero_rows
            buffer[half, PAD:, :] = bits_ref[half, q - 1].astype(jnp.float32)
            head_ref[q, :, lanes] = buffer[half, PAD : 2 * PAD, :]
            tail_ref[q, :, lanes] = buffer[half, token_count:, :]

        def emit_one(j, row):
            gated_ref[j, :, lanes] = row

        def emit_gate(j, row):
            gated = rounded(gated_ref[j, :, lanes] * row)
            if j < halo_rows:
                gated = gated * keep
            gated_ref[j, :, lanes] = gated

        filter_chunks(one_ref.at[half], [spread(taps_ref[1, i : i + 1, lanes]) for i in range(tap_count)], length, emit_one)
        filter_chunks(two_ref.at[half], [spread(taps_ref[2, i : i + 1, lanes]) for i in range(tap_count)], length, emit_gate)
        if half == 0:
            for copy in late:
                copy.wait()
            head_ref[0] = head_bits_ref[...].astype(jnp.float32)[:PAD]
            tail_ref[0] = tail_bits_ref[...].astype(jnp.float32)[edge_rows - PAD :]
            scale_ref[...] = residues_ref[...] * jnp.sqrt(one_minus_exp(2.0 * rates_ref[...]))
        rates = rates_ref[:, lanes]
        decay = jnp.exp(-rates)
        decays = [spread(decay[m : m + 1]) for m in range(mode_count)]
        states = [gated_ref[0, :, lanes]] * mode_count
        for j in range(1, length):
            row = gated_ref[j, :, lanes]
            states = [d * h + row for d, h in zip(decays, states)]
        for m in range(mode_count):
            ends_ref[m, :, lanes] = states[m]
            weight = jnp.exp(spread(rates[m : m + 1]) * to_end)
            state_ref[m : m + 1, lanes] = jnp.sum(weight * states[m], axis=0, keepdims=True)


def local_kernel(
    rates_ref, scale_ref, taps_ref, zeroth_ref, gated_ref, local_ref, gate_ref, buffer_ref
):
    length = zeroth_ref.shape[1] // CHUNKS
    mode_count = rates_ref.shape[0]
    tap_count = taps_ref.shape[1]
    buffer_ref[0:PAD, :] = jnp.zeros((PAD, LANES), jnp.float32)
    buffer_ref[PAD:, :] = zeroth_ref[0].astype(jnp.float32)

    def emit(j, row):
        gate_ref[j] = row

    filter_chunks(buffer_ref, [spread(taps_ref[0, i : i + 1, :]) for i in range(tap_count)], length, emit)
    decay = jnp.exp(-rates_ref[...])
    decays = [spread(decay[m : m + 1]) for m in range(mode_count)]
    scales = [spread(scale_ref[m : m + 1, :]) for m in range(mode_count)]
    states = [gated_ref[0]] * mode_count
    for j in range(length):
        if j > 0:
            row = gated_ref[j]
            states = [d * h + row for d, h in zip(decays, states)]
        local_ref[j] = pairwise_sum([c * h for c, h in zip(scales, states)])


def final_kernel(
    rates_ref, scale_ref, taps_ref, skip_ref, incoming_ref, halo_ref, head_ref, ends_ref, gated_ref, local_ref,
    gate_ref, out_ref, edge_ref, rows_ref,
):
    length = gated_ref.shape[0]
    mode_count = rates_ref.shape[0]
    tap_count = taps_ref.shape[1]
    halo_rows = tap_count - 1
    sublane = lax.broadcasted_iota(jnp.int32, (CHUNKS, LANES), 0)
    edges = []
    for q in range(3):
        edge_ref[q, 0:PAD, :] = halo_ref[q]
        edge_ref[q, PAD : 2 * PAD, :] = head_ref[q, 0:PAD, :]
        edges.append(
            pairwise_sum([taps_ref[q, i : i + 1, :] * edge_ref[q, PAD - i : 2 * PAD - i, :] for i in range(tap_count)])
        )
    edge_gated = rounded(edges[1] * edges[2]) * jnp.where(lax.axis_index("seq") == 0, 0.0, 1.0)
    rates = rates_ref[...]
    scale = scale_ref[...]
    decay = jnp.exp(-rates)
    edge_state = jnp.zeros_like(decay)
    for t in range(halo_rows):
        edge_state = decay * edge_state + edge_gated[t : t + 1]
    edge_state = edge_state * jnp.exp(-rates * float(length - halo_rows))
    chunk_decay = jnp.exp(-rates * float(length))
    decays = [spread(decay[m : m + 1]) for m in range(mode_count)]
    states = []
    for m in range(mode_count):
        factor = spread(chunk_decay[m : m + 1])
        ends = ends_ref[m] + jnp.where(sublane == 0, spread(edge_state[m : m + 1]), 0.0)
        carried = jnp.where(sublane == 0, spread(incoming_ref[m : m + 1, :]), pltpu.roll(ends, 1, 0))
        for distance in (1, 2, 4):
            carried = carried + jnp.where(sublane >= distance, factor * pltpu.roll(carried, distance, 0), 0.0)
            factor = factor * factor
        states.append(carried * spread(scale[m : m + 1]))
    skip = spread(skip_ref[...])
    for j in range(length):
        states = [d * h for d, h in zip(decays, states)]
        gated, gate = gated_ref[j], gate_ref[j]
        if j < halo_rows:
            new = jnp.where(sublane == 0, spread(edge_gated[j : j + 1]), 0.0)
            states = [h + spread(scale[m : m + 1]) * new for m, h in enumerate(states)]
            gated = gated + new
            gate = jnp.where(sublane == 0, spread(edges[0][j : j + 1]), gate)
        long_out = rounded(local_ref[j] + pairwise_sum(states))
        rows_ref[pl.ds(j, CHUNKS, stride=length), :] = gate * (long_out + skip * gated)
    out_ref[...] = rows_ref[...].astype(jnp.bfloat16)


def by_lanes(*dims):
    return pl.BlockSpec((*dims, LANES), lambda i: (*(0 for _ in dims), i))


def one_projection(q, tokens):
    return pl.BlockSpec((1, tokens, LANES), lambda i: (q, 0, i))


def shape32(*dims):
    return jax.ShapeDtypeStruct(dims, jnp.float32)


PARAMS = pltpu.CompilerParams(vmem_limit_bytes=24 * 1024 * 1024)


def on_device(projections, taps, rates, residues, skip):
    tap_count = taps.shape[0]
    halo_rows = tap_count - 1
    _, tokens, channels = projections.shape
    mode_count = rates.shape[1]
    length = tokens // CHUNKS
    grid = (channels // LANES,)
    halves = channels // LANES
    count = lax.axis_size("seq")
    index = lax.axis_index("seq")
    taps = taps.transpose(1, 0, 2)
    hbm = pl.BlockSpec(memory_space=pltpu.HBM)
    vmem = pl.BlockSpec(memory_space=pltpu.VMEM)
    gated, ends, state, head, tail, rates_own, scale, taps, skip = pl.pallas_call(
        state_kernel,
        out_shape=(
            shape32(length, CHUNKS, channels),
            shape32(mode_count, CHUNKS, channels),
            shape32(mode_count, channels),
            shape32(3, PAD, channels),
            shape32(3, PAD, channels),
            shape32(mode_count, channels),
            shape32(mode_count, channels),
            shape32(3, tap_count, channels),
            shape32(1, channels),
        ),
        in_specs=[hbm] * 5,
        out_specs=(vmem,) * 9,
        scratch_shapes=[
            pltpu.VMEM((halves, 2, tokens, LANES), jnp.bfloat16),
            pltpu.VMEM((2 * PAD, channels), jnp.bfloat16),
            pltpu.VMEM((2 * PAD, channels), jnp.bfloat16),
            pltpu.VMEM((mode_count, channels), jnp.float32),
            pltpu.VMEM((halves, PAD + tokens, LANES), jnp.float32),
            pltpu.VMEM((halves, PAD + tokens, LANES), jnp.float32),
            pltpu.SemaphoreType.DMA((2 * halves + 6,)),
        ],
        compiler_params=PARAMS,
        name="state",
    )(*(
        pltpu.with_memory_space_constraint(array, pltpu.HBM)
        for array in (rates.T, residues.T, taps, skip[None, :], projections)
    ))
    taps_spec = by_lanes(3, tap_count)
    modes_spec = by_lanes(mode_count)
    grid_spec = by_lanes(length, CHUNKS)
    ends_spec = by_lanes(mode_count, CHUNKS)
    local, gate = pl.pallas_call(
        local_kernel,
        out_shape=(shape32(length, CHUNKS, channels),) * 2,
        grid=grid,
        in_specs=[modes_spec, modes_spec, taps_spec, one_projection(0, tokens), grid_spec],
        out_specs=(grid_spec, grid_spec),
        scratch_shapes=[pltpu.VMEM((PAD + tokens, LANES), jnp.float32)],
        compiler_params=PARAMS,
        name="local",
    )(rates_own, scale, taps, projections, gated)

    def decayed(steps):
        return jnp.exp(-rates_own * jnp.asarray(steps, jnp.float32))

    def pack(state, first, last):
        high = lax.reduce_precision(state, 8, 7)
        rows = [high, state - high, last.reshape(3 * PAD, channels), first.reshape(2 * PAD, channels)]
        return jnp.concatenate(rows, axis=0).astype(jnp.bfloat16)

    def unpack(packed):
        packed = packed.astype(jnp.float32)
        edges = packed[2 * mode_count :].reshape(5, PAD, channels)
        return packed[:mode_count] + packed[mode_count : 2 * mode_count], edges[3:], edges[:3]

    def send(packed, flip, devices):
        return lax.ppermute(packed, "seq", [(i, i ^ flip) for i in devices])

    def edge_state_of(left_last, right_first):
        joined = jnp.concatenate([left_last[1:], right_first], axis=1)
        edge = sum(taps[1:, i, None, :] * joined[:, PAD - i : 2 * PAD - i, :] for i in range(tap_count))
        gates = rounded(edge[0] * edge[1])
        edge_state = jnp.zeros_like(state)
        for t in range(halo_rows):
            edge_state = decayed(1.0) * edge_state + gates[t][None, :]
        return edge_state

    def arriving(left_state, edge_state, size):
        offset = (index % size * tokens).astype(jnp.float32)
        edge_part = decayed(jnp.maximum(offset - halo_rows, 0.0)) * edge_state
        return decayed(offset) * left_state + jnp.where(index % size == 0, 0.0, edge_part)

    def join(block, received, prefix, halo, size):
        state, first, last = block
        other_state, other_first, other_last = unpack(received)
        is_right = index // size % 2 == 1
        left_last = jnp.where(is_right, other_last, last)
        right_first = jnp.where(is_right, first, other_first)
        left_state = jnp.where(is_right, other_state, state)
        right_state = jnp.where(is_right, state, other_state)
        edge_state = edge_state_of(left_last, right_first)
        prefix = jnp.where(is_right, prefix + arriving(left_state, edge_state, size), prefix)
        halo = jnp.where(is_right & (index % size == 0), other_last, halo)
        steps = float(size * tokens)
        state = right_state + decayed(steps - halo_rows) * edge_state + decayed(steps) * left_state
        first = jnp.where(is_right, other_first, first)
        last = jnp.where(is_right, last, other_last)
        return (state, first, last), prefix, halo

    everyone, early, late = range(count), range(count // 2), range(count // 2, count)
    block, prefix, halo = (state, head[1:], tail), jnp.zeros_like(state), jnp.zeros_like(tail)
    block, prefix, halo = join(block, send(pack(*block), 1, everyone), prefix, halo, 1)
    received = send(pack(*block), 3, everyone)
    received, local, gate = lax.optimization_barrier((received, local, gate))
    block, prefix, halo = join(block, received, prefix, halo, 2)
    packed = pack(*block)
    received = send(packed, 5, early)
    joined, _, _ = join(block, received, prefix, halo, 4)
    total = pack(*joined)
    crossed = send(total, 13, early)
    left_state, _, left_last = unpack(crossed)
    offset = (index % (count // 2) * tokens).astype(jnp.float32)
    is_late = index >= count // 2
    prefix = prefix + jnp.where(is_late, decayed(offset), 0.0) * left_state
    second, prefix, left_last = lax.optimization_barrier((send(packed, 5, late), prefix, left_last))
    (_, first, _), prefix, halo = join(block, received + second, prefix, halo, 4)
    edge_part = decayed(jnp.maximum(offset - halo_rows, 0.0)) * edge_state_of(left_last, first)
    prefix = prefix + jnp.where(index > count // 2, edge_part, 0.0)
    halo = jnp.where(index == count // 2, left_last, halo)
    return pl.pallas_call(
        final_kernel,
        out_shape=jax.ShapeDtypeStruct((tokens, channels), jnp.bfloat16),
        grid=grid,
        in_specs=[
            modes_spec, modes_spec, taps_spec, by_lanes(1), modes_spec, by_lanes(3, PAD), by_lanes(3, PAD),
            ends_spec, grid_spec, grid_spec, grid_spec,
        ],
        out_specs=by_lanes(tokens),
        scratch_shapes=[
            pltpu.VMEM((3, 2 * PAD, LANES), jnp.float32),
            pltpu.VMEM((tokens, LANES), jnp.float32),
        ],
        compiler_params=PARAMS,
        name="final",
    )(rates_own, scale, taps, skip, prefix, halo, head, ends, gated, local, gate)


def solution(mesh):
    in_specs = (P(None, "seq", "fft"), P(None, None, "fft"), P(), P(), P("fft"))
    out_specs = P("seq", "fft")
    return jax.shard_map(on_device, mesh=mesh, in_specs=in_specs, out_specs=out_specs, check_vma=False)
```

```python
import jax
import jax.numpy as jnp
from jax import lax
from jax.experimental import pallas as pl
from jax.experimental.pallas import tpu as pltpu
from jax.sharding import PartitionSpec as P

CHUNKS = 8
LANES = 128
PAD = 8


def rounded(values):
    return values.astype(jnp.bfloat16).astype(jnp.float32)


def spread(row):
    return jnp.broadcast_to(row, (CHUNKS, row.shape[-1]))


def pairwise_sum(terms):
    while len(terms) > 1:
        joined = [a + b for a, b in zip(terms[0::2], terms[1::2])]
        terms = joined + ([terms[-1]] if len(terms) % 2 else [])
    return terms[0]


def one_minus_exp(y):
    series = jnp.ones_like(y)
    for divisor in (7.0, 6.0, 5.0, 4.0, 3.0, 2.0):
        series = 1.0 - y * (1.0 / divisor) * series
    return jnp.where(y < 0.1, y * series, 1.0 - jnp.exp(-y))


def chunk_rows(buffer, first, count, stride):
    return [buffer[pl.ds(PAD + first + k, CHUNKS, stride=stride), :] for k in range(count)]


def filter_chunks(buffer, taps, length, emit):
    tap_count = len(taps)
    step = 8
    for first in range(0, length, step):
        rows = chunk_rows(buffer, first - (tap_count - 1), step + tap_count - 1, length)
        for k in range(step):
            terms = [taps[i] * rows[k + tap_count - 1 - i] for i in range(tap_count)]
            emit(first + k, pairwise_sum(terms))


def state_kernel(
    rates_hbm, residues_hbm, taps_hbm, skip_hbm, tokens_hbm,
    gated_ref, ends_ref, state_ref, head_ref, tail_ref, rates_ref, scale_ref, taps_ref, skip_ref,
    bits_ref, head_bits_ref, tail_bits_ref, residues_ref, one_ref, two_ref, sems,
):
    channels = rates_ref.shape[1]
    mode_count = rates_ref.shape[0]
    token_count = bits_ref.shape[2]
    length = token_count // CHUNKS
    tap_count = taps_ref.shape[1]
    halo_rows = tap_count - 1
    halves = channels // LANES
    edge_rows = head_bits_ref.shape[0]
    start = pl.multiple_of(lax.axis_index("fft") * channels, channels)
    loads = []
    for half in range(halves):
        for q in (1, 2):
            copy = pltpu.make_async_copy(
                tokens_hbm.at[q, :, pl.ds(half * LANES, LANES)], bits_ref.at[half, q - 1], sems.at[2 * half + q - 1]
            )
            copy.start()
            loads.append(copy)
    early = [
        pltpu.make_async_copy(taps_hbm, taps_ref, sems.at[2 * halves + 4]),
        pltpu.make_async_copy(skip_hbm, skip_ref, sems.at[2 * halves + 5]),
    ]
    late = [
        pltpu.make_async_copy(rates_hbm.at[:, pl.ds(start, channels)], rates_ref, sems.at[2 * halves]),
        pltpu.make_async_copy(residues_hbm.at[:, pl.ds(start, channels)], residues_ref, sems.at[2 * halves + 1]),
        pltpu.make_async_copy(tokens_hbm.at[0, 0:edge_rows, :], head_bits_ref, sems.at[2 * halves + 2]),
        pltpu.make_async_copy(
            tokens_hbm.at[0, token_count - edge_rows : token_count, :], tail_bits_ref, sems.at[2 * halves + 3]
        ),
    ]
    for copy in early + late:
        copy.start()
    sublane = lax.broadcasted_iota(jnp.int32, (CHUNKS, LANES), 0)
    keep = jnp.where(sublane == 0, jnp.where(lax.axis_index("seq") == 0, 1.0, 0.0), 1.0)
    to_end = -((CHUNKS - 1 - sublane) * length).astype(jnp.float32)
    zero_rows = jnp.zeros((PAD, LANES), jnp.float32)
    for copy in early:
        copy.wait()
    for half in range(halves):
        lanes = slice(half * LANES, (half + 1) * LANES)
        for buffer, q in ((one_ref, 1), (two_ref, 2)):
            loads[2 * half + q - 1].wait()
            buffer[half, 0:PAD, :] = zero_rows
            buffer[half, PAD:, :] = bits_ref[half, q - 1].astype(jnp.float32)
            head_ref[q, :, lanes] = buffer[half, PAD : 2 * PAD, :]
            tail_ref[q, :, lanes] = buffer[half, token_count:, :]

        def emit_one(j, row):
            gated_ref[j, :, lanes] = row

        def emit_gate(j, row):
            gated = rounded(gated_ref[j, :, lanes] * row)
            if j < halo_rows:
                gated = gated * keep
            gated_ref[j, :, lanes] = gated

        filter_chunks(one_ref.at[half], [spread(taps_ref[1, i : i + 1, lanes]) for i in range(tap_count)], length, emit_one)
        filter_chunks(two_ref.at[half], [spread(taps_ref[2, i : i + 1, lanes]) for i in range(tap_count)], length, emit_gate)
        if half == 0:
            for copy in late:
                copy.wait()
            head_ref[0] = head_bits_ref[...].astype(jnp.float32)[:PAD]
            tail_ref[0] = tail_bits_ref[...].astype(jnp.float32)[edge_rows - PAD :]
            scale_ref[...] = residues_ref[...] * jnp.sqrt(one_minus_exp(2.0 * rates_ref[...]))
        rates = rates_ref[:, lanes]
        decay = jnp.exp(-rates)
        decays = [spread(decay[m : m + 1]) for m in range(mode_count)]
        states = [gated_ref[0, :, lanes]] * mode_count
        for j in range(1, length):
            row = gated_ref[j, :, lanes]
            states = [d * h + row for d, h in zip(decays, states)]
        for m in range(mode_count):
            ends_ref[m, :, lanes] = states[m]
            weight = jnp.exp(spread(rates[m : m + 1]) * to_end)
            state_ref[m : m + 1, lanes] = jnp.sum(weight * states[m], axis=0, keepdims=True)


def local_kernel(rates_ref, scale_ref, taps_ref, tokens_ref, gated_ref, local_ref, gate_ref, buffer_ref):
    length = gated_ref.shape[0]
    mode_count = rates_ref.shape[0]
    tap_count = taps_ref.shape[1]
    for half in range(rates_ref.shape[1] // LANES):
        lanes = slice(half * LANES, (half + 1) * LANES)
        buffer_ref[half, 0:PAD, :] = jnp.zeros((PAD, LANES), jnp.float32)
        buffer_ref[half, PAD:, :] = tokens_ref[0, :, lanes].astype(jnp.float32)

        def emit(j, row):
            gate_ref[j, :, lanes] = row

        rows = [spread(taps_ref[0, i : i + 1, lanes]) for i in range(tap_count)]
        filter_chunks(buffer_ref.at[half], rows, length, emit)
        decay = jnp.exp(-rates_ref[:, lanes])
        decays = [spread(decay[m : m + 1]) for m in range(mode_count)]
        scales = [spread(scale_ref[m : m + 1, lanes]) for m in range(mode_count)]
        states = [gated_ref[0, :, lanes]] * mode_count
        for j in range(length):
            if j > 0:
                row = gated_ref[j, :, lanes]
                states = [d * h + row for d, h in zip(decays, states)]
            local_ref[j, :, lanes] = pairwise_sum([c * h for c, h in zip(scales, states)])


def late_kernel(*refs):
    operands, rest = refs[:11], refs[12:]

    @pl.when(lax.axis_index("seq") >= lax.axis_size("seq") // 2)
    def _():
        final_kernel(*operands, *rest)


def final_kernel(
    rates_ref, scale_ref, taps_ref, skip_ref, incoming_ref, halo_ref, head_ref, ends_ref, gated_ref, local_ref,
    gate_ref, out_hbm, edge_ref, rows_ref, out_ref, sems,
):
    length = gated_ref.shape[0]
    mode_count = rates_ref.shape[0]
    tap_count = taps_ref.shape[1]
    halo_rows = tap_count - 1
    sublane = lax.broadcasted_iota(jnp.int32, (CHUNKS, LANES), 0)
    is_new = jnp.where(lax.axis_index("seq") == 0, 0.0, 1.0)
    copies = []
    for half in range(rates_ref.shape[1] // LANES):
        lanes = slice(half * LANES, (half + 1) * LANES)
        edges = []
        for q in range(3):
            edge_ref[q, 0:PAD, :] = halo_ref[q, :, lanes]
            edge_ref[q, PAD : 2 * PAD, :] = head_ref[q, :, lanes]
            terms = [taps_ref[q, i : i + 1, lanes] * edge_ref[q, PAD - i : 2 * PAD - i, :] for i in range(tap_count)]
            edges.append(pairwise_sum(terms))
        edge_gated = rounded(edges[1] * edges[2]) * is_new
        rates = rates_ref[:, lanes]
        scale = scale_ref[:, lanes]
        decay = jnp.exp(-rates)
        edge_state = jnp.zeros_like(decay)
        for t in range(halo_rows):
            edge_state = decay * edge_state + edge_gated[t : t + 1]
        edge_state = edge_state * jnp.exp(-rates * float(length - halo_rows))
        chunk_decay = jnp.exp(-rates * float(length))
        decays = [spread(decay[m : m + 1]) for m in range(mode_count)]
        states = []
        for m in range(mode_count):
            factor = spread(chunk_decay[m : m + 1])
            ends = ends_ref[m, :, lanes] + jnp.where(sublane == 0, spread(edge_state[m : m + 1]), 0.0)
            carried = jnp.where(sublane == 0, spread(incoming_ref[m : m + 1, lanes]), pltpu.roll(ends, 1, 0))
            for distance in (1, 2, 4):
                carried = carried + jnp.where(sublane >= distance, factor * pltpu.roll(carried, distance, 0), 0.0)
                factor = factor * factor
            states.append(carried * spread(scale[m : m + 1]))
        skip = spread(skip_ref[:, lanes])
        for j in range(length):
            states = [d * h for d, h in zip(decays, states)]
            gated, gate = gated_ref[j, :, lanes], gate_ref[j, :, lanes]
            if j < halo_rows:
                new = jnp.where(sublane == 0, spread(edge_gated[j : j + 1]), 0.0)
                states = [h + spread(scale[m : m + 1]) * new for m, h in enumerate(states)]
                gated = gated + new
                gate = jnp.where(sublane == 0, spread(edges[0][j : j + 1]), gate)
            long_out = rounded(local_ref[j, :, lanes] + pairwise_sum(states))
            rows_ref[half, pl.ds(j, CHUNKS, stride=length), :] = gate * (long_out + skip * gated)
        out_ref[half] = rows_ref[half].astype(jnp.bfloat16)
        copies.append(pltpu.make_async_copy(out_ref.at[half], out_hbm.at[:, pl.ds(half * LANES, LANES)], sems.at[half]))
        copies[-1].start()
    for copy in copies:
        copy.wait()


def shape32(*dims):
    return jax.ShapeDtypeStruct(dims, jnp.float32)


PARAMS = pltpu.CompilerParams(vmem_limit_bytes=24 * 1024 * 1024)


def on_device(projections, taps, rates, residues, skip):
    tap_count = taps.shape[0]
    halo_rows = tap_count - 1
    _, tokens, channels = projections.shape
    mode_count = rates.shape[1]
    length = tokens // CHUNKS
    halves = channels // LANES
    count = lax.axis_size("seq")
    index = lax.axis_index("seq")
    taps = taps.transpose(1, 0, 2)
    hbm = pl.BlockSpec(memory_space=pltpu.HBM)
    vmem = pl.BlockSpec(memory_space=pltpu.VMEM)
    gated, ends, state, head, tail, rates_own, scale, taps, skip = pl.pallas_call(
        state_kernel,
        out_shape=(
            shape32(length, CHUNKS, channels),
            shape32(mode_count, CHUNKS, channels),
            shape32(mode_count, channels),
            shape32(3, PAD, channels),
            shape32(3, PAD, channels),
            shape32(mode_count, channels),
            shape32(mode_count, channels),
            shape32(3, tap_count, channels),
            shape32(1, channels),
        ),
        in_specs=[hbm] * 5,
        out_specs=(vmem,) * 9,
        scratch_shapes=[
            pltpu.VMEM((halves, 2, tokens, LANES), jnp.bfloat16),
            pltpu.VMEM((2 * PAD, channels), jnp.bfloat16),
            pltpu.VMEM((2 * PAD, channels), jnp.bfloat16),
            pltpu.VMEM((mode_count, channels), jnp.float32),
            pltpu.VMEM((halves, PAD + tokens, LANES), jnp.float32),
            pltpu.VMEM((halves, PAD + tokens, LANES), jnp.float32),
            pltpu.SemaphoreType.DMA((2 * halves + 6,)),
        ],
        compiler_params=PARAMS,
        name="state",
    )(*(
        pltpu.with_memory_space_constraint(array, pltpu.HBM)
        for array in (rates.T, residues.T, taps, skip[None, :], projections)
    ))
    local, gate = pl.pallas_call(
        local_kernel,
        out_shape=(shape32(length, CHUNKS, channels),) * 2,
        in_specs=[vmem] * 5,
        out_specs=(vmem, vmem),
        scratch_shapes=[pltpu.VMEM((halves, PAD + tokens, LANES), jnp.float32)],
        compiler_params=PARAMS,
        name="local",
    )(rates_own, scale, taps, projections, gated)

    def decayed(steps):
        return jnp.exp(-rates_own * jnp.asarray(steps, jnp.float32))

    def pack(state, first, last):
        high = lax.reduce_precision(state, 8, 7)
        rows = [high, state - high, last.reshape(3 * PAD, channels), first.reshape(2 * PAD, channels)]
        return jnp.concatenate(rows, axis=0).astype(jnp.bfloat16)

    def unpack(packed):
        packed = packed.astype(jnp.float32)
        edges = packed[2 * mode_count :].reshape(5, PAD, channels)
        return packed[:mode_count] + packed[mode_count : 2 * mode_count], edges[3:], edges[:3]

    def send(packed, flip, devices):
        return lax.ppermute(packed, "seq", [(i, i ^ flip) for i in devices])

    def edge_state_of(left_last, right_first):
        joined = jnp.concatenate([left_last[1:], right_first], axis=1)
        edge = sum(taps[1:, i, None, :] * joined[:, PAD - i : 2 * PAD - i, :] for i in range(tap_count))
        gates = rounded(edge[0] * edge[1])
        edge_state = jnp.zeros_like(state)
        for t in range(halo_rows):
            edge_state = decayed(1.0) * edge_state + gates[t][None, :]
        return edge_state

    def arriving(left_state, edge_state, size):
        offset = (index % size * tokens).astype(jnp.float32)
        edge_part = decayed(jnp.maximum(offset - halo_rows, 0.0)) * edge_state
        return decayed(offset) * left_state + jnp.where(index % size == 0, 0.0, edge_part)

    def join(block, received, prefix, halo, size):
        state, first, last = block
        other_state, other_first, other_last = unpack(received)
        is_right = index // size % 2 == 1
        left_last = jnp.where(is_right, other_last, last)
        right_first = jnp.where(is_right, first, other_first)
        left_state = jnp.where(is_right, other_state, state)
        right_state = jnp.where(is_right, state, other_state)
        edge_state = edge_state_of(left_last, right_first)
        prefix = jnp.where(is_right, prefix + arriving(left_state, edge_state, size), prefix)
        halo = jnp.where(is_right & (index % size == 0), other_last, halo)
        steps = float(size * tokens)
        state = right_state + decayed(steps - halo_rows) * edge_state + decayed(steps) * left_state
        first = jnp.where(is_right, other_first, first)
        last = jnp.where(is_right, last, other_last)
        return (state, first, last), prefix, halo

    def finish(kernel, prefix, halo, *earlier):
        operands = (rates_own, scale, taps, skip, prefix, halo, head, ends, gated, local, gate)
        return pl.pallas_call(
            kernel,
            out_shape=jax.ShapeDtypeStruct((tokens, channels), jnp.bfloat16),
            in_specs=[vmem] * len(operands) + [hbm] * len(earlier),
            out_specs=hbm,
            scratch_shapes=[
                pltpu.VMEM((3, 2 * PAD, LANES), jnp.float32),
                pltpu.VMEM((halves, tokens, LANES), jnp.float32),
                pltpu.VMEM((halves, tokens, LANES), jnp.bfloat16),
                pltpu.SemaphoreType.DMA((halves,)),
            ],
            input_output_aliases={len(operands): 0} if earlier else {},
            cost_estimate=pl.CostEstimate(flops=10_000_000, bytes_accessed=2_000_000, transcendentals=0),
            compiler_params=PARAMS,
            name="final",
        )(*operands, *earlier)

    everyone, early, late = range(count), range(count // 2), range(count // 2, count)
    block, prefix, halo = (state, head[1:], tail), jnp.zeros_like(state), jnp.zeros_like(tail)
    block, prefix, halo = join(block, send(pack(*block), 1, everyone), prefix, halo, 1)
    received = send(pack(*block), 3, everyone)
    received, local, gate = lax.optimization_barrier((received, local, gate))
    block, prefix, halo = join(block, received, prefix, halo, 2)
    packed = pack(*block)
    received = lax.ppermute(packed, "seq", [(i, i ^ (5 if i in early else 1)) for i in everyone])
    joined, early_prefix, early_halo = join(block, received, prefix, halo, 4)
    out = finish(final_kernel, early_prefix, early_halo)
    total = pack(*joined)
    crossed = send(total, 13, early)
    crossed, out = lax.optimization_barrier((crossed, out))
    left_state, _, left_last = unpack(crossed)
    offset = (index % (count // 2) * tokens).astype(jnp.float32)
    is_late = index >= count // 2
    prefix = prefix + jnp.where(is_late, decayed(offset), 0.0) * left_state
    second, prefix, left_last = lax.optimization_barrier(
        (lax.ppermute(packed, "seq", [(i, i ^ (5 if i in late else 1)) for i in everyone]), prefix, left_last)
    )
    (_, first, _), prefix, halo = join(block, jnp.where(is_late, second, received), prefix, halo, 4)
    edge_part = decayed(jnp.maximum(offset - halo_rows, 0.0)) * edge_state_of(left_last, first)
    prefix = prefix + jnp.where(index > count // 2, edge_part, 0.0)
    halo = jnp.where(index == count // 2, left_last, halo)
    return finish(late_kernel, prefix, halo, out)


def solution(mesh):
    in_specs = (P(None, "seq", "fft"), P(None, None, "fft"), P(), P(), P("fft"))
    out_specs = P("seq", "fft")
    return jax.shard_map(on_device, mesh=mesh, in_specs=in_specs, out_specs=out_specs, check_vma=False)
```

```python
import jax
import jax.numpy as jnp
from jax import lax
from jax.experimental import pallas as pl
from jax.experimental.pallas import tpu as pltpu
from jax.sharding import PartitionSpec as P

CHUNKS = 8
CROSSING = {0: 12, 1: 15, 2: 14, 3: 13, 4: 9, 5: 8, 6: 11, 7: 10}
LANES = 128
PAD = 8


def rounded(values):
    return values.astype(jnp.bfloat16).astype(jnp.float32)


def spread(row):
    return jnp.broadcast_to(row, (CHUNKS, row.shape[-1]))


def pairwise_sum(terms):
    while len(terms) > 1:
        joined = [a + b for a, b in zip(terms[0::2], terms[1::2])]
        terms = joined + ([terms[-1]] if len(terms) % 2 else [])
    return terms[0]


def one_minus_exp(y):
    series = jnp.ones_like(y)
    for divisor in (7.0, 6.0, 5.0, 4.0, 3.0, 2.0):
        series = 1.0 - y * (1.0 / divisor) * series
    return jnp.where(y < 0.1, y * series, 1.0 - jnp.exp(-y))


def chunk_rows(buffer, first, count, stride):
    return [buffer[pl.ds(PAD + first + k, CHUNKS, stride=stride), :] for k in range(count)]


def filter_chunks(buffer, taps, length, emit):
    tap_count = len(taps)
    step = 8
    for first in range(0, length, step):
        rows = chunk_rows(buffer, first - (tap_count - 1), step + tap_count - 1, length)
        for k in range(step):
            terms = [taps[i] * rows[k + tap_count - 1 - i] for i in range(tap_count)]
            emit(first + k, pairwise_sum(terms))


def state_kernel(
    rates_hbm, residues_hbm, taps_hbm, skip_hbm, tokens_hbm,
    gated_ref, ends_ref, state_ref, head_ref, tail_ref, rates_ref, scale_ref, taps_ref, skip_ref,
    bits_ref, head_bits_ref, tail_bits_ref, residues_ref, one_ref, two_ref, sems,
):
    channels = rates_ref.shape[1]
    mode_count = rates_ref.shape[0]
    token_count = bits_ref.shape[2]
    length = token_count // CHUNKS
    tap_count = taps_ref.shape[1]
    halo_rows = tap_count - 1
    halves = channels // LANES
    edge_rows = head_bits_ref.shape[0]
    start = pl.multiple_of(lax.axis_index("fft") * channels, channels)
    loads = []
    for half in range(halves):
        for q in (1, 2):
            copy = pltpu.make_async_copy(
                tokens_hbm.at[q, :, pl.ds(half * LANES, LANES)], bits_ref.at[half, q - 1], sems.at[2 * half + q - 1]
            )
            copy.start()
            loads.append(copy)
    early = [
        pltpu.make_async_copy(taps_hbm, taps_ref, sems.at[2 * halves + 4]),
        pltpu.make_async_copy(skip_hbm, skip_ref, sems.at[2 * halves + 5]),
    ]
    late = [
        pltpu.make_async_copy(rates_hbm.at[:, pl.ds(start, channels)], rates_ref, sems.at[2 * halves]),
        pltpu.make_async_copy(residues_hbm.at[:, pl.ds(start, channels)], residues_ref, sems.at[2 * halves + 1]),
        pltpu.make_async_copy(tokens_hbm.at[0, 0:edge_rows, :], head_bits_ref, sems.at[2 * halves + 2]),
        pltpu.make_async_copy(
            tokens_hbm.at[0, token_count - edge_rows : token_count, :], tail_bits_ref, sems.at[2 * halves + 3]
        ),
    ]
    for copy in early + late:
        copy.start()
    sublane = lax.broadcasted_iota(jnp.int32, (CHUNKS, LANES), 0)
    keep = jnp.where(sublane == 0, jnp.where(lax.axis_index("seq") == 0, 1.0, 0.0), 1.0)
    to_end = -((CHUNKS - 1 - sublane) * length).astype(jnp.float32)
    zero_rows = jnp.zeros((PAD, LANES), jnp.float32)
    for copy in early:
        copy.wait()
    for half in range(halves):
        lanes = slice(half * LANES, (half + 1) * LANES)
        for buffer, q in ((one_ref, 1), (two_ref, 2)):
            loads[2 * half + q - 1].wait()
            buffer[half, 0:PAD, :] = zero_rows
            buffer[half, PAD:, :] = bits_ref[half, q - 1].astype(jnp.float32)
            head_ref[q, :, lanes] = buffer[half, PAD : 2 * PAD, :]
            tail_ref[q, :, lanes] = buffer[half, token_count:, :]

        def emit_one(j, row):
            gated_ref[j, :, lanes] = row

        def emit_gate(j, row):
            gated = rounded(gated_ref[j, :, lanes] * row)
            if j < halo_rows:
                gated = gated * keep
            gated_ref[j, :, lanes] = gated

        filter_chunks(one_ref.at[half], [spread(taps_ref[1, i : i + 1, lanes]) for i in range(tap_count)], length, emit_one)
        filter_chunks(two_ref.at[half], [spread(taps_ref[2, i : i + 1, lanes]) for i in range(tap_count)], length, emit_gate)
        if half == 0:
            for copy in late:
                copy.wait()
            head_ref[0] = head_bits_ref[...].astype(jnp.float32)[:PAD]
            tail_ref[0] = tail_bits_ref[...].astype(jnp.float32)[edge_rows - PAD :]
            scale_ref[...] = residues_ref[...] * jnp.sqrt(one_minus_exp(2.0 * rates_ref[...]))
        rates = rates_ref[:, lanes]
        decay = jnp.exp(-rates)
        decays = [spread(decay[m : m + 1]) for m in range(mode_count)]
        states = [gated_ref[0, :, lanes]] * mode_count
        for j in range(1, length):
            row = gated_ref[j, :, lanes]
            states = [d * h + row for d, h in zip(decays, states)]
        for m in range(mode_count):
            ends_ref[m, :, lanes] = states[m]
            weight = jnp.exp(spread(rates[m : m + 1]) * to_end)
            state_ref[m : m + 1, lanes] = jnp.sum(weight * states[m], axis=0, keepdims=True)


def local_kernel(rates_ref, scale_ref, taps_ref, tokens_ref, gated_ref, local_ref, gate_ref, buffer_ref):
    length = gated_ref.shape[0]
    mode_count = rates_ref.shape[0]
    tap_count = taps_ref.shape[1]
    for half in range(rates_ref.shape[1] // LANES):
        lanes = slice(half * LANES, (half + 1) * LANES)
        buffer_ref[half, 0:PAD, :] = jnp.zeros((PAD, LANES), jnp.float32)
        buffer_ref[half, PAD:, :] = tokens_ref[0, :, lanes].astype(jnp.float32)

        def emit(j, row):
            gate_ref[j, :, lanes] = row

        rows = [spread(taps_ref[0, i : i + 1, lanes]) for i in range(tap_count)]
        filter_chunks(buffer_ref.at[half], rows, length, emit)
        decay = jnp.exp(-rates_ref[:, lanes])
        decays = [spread(decay[m : m + 1]) for m in range(mode_count)]
        scales = [spread(scale_ref[m : m + 1, lanes]) for m in range(mode_count)]
        states = [gated_ref[0, :, lanes]] * mode_count
        for j in range(length):
            if j > 0:
                row = gated_ref[j, :, lanes]
                states = [d * h + row for d, h in zip(decays, states)]
            local_ref[j, :, lanes] = pairwise_sum([c * h for c, h in zip(scales, states)])


def late_kernel(*refs):
    operands, rest = refs[:11], refs[12:]

    @pl.when(lax.axis_index("seq") >= lax.axis_size("seq") // 2)
    def _():
        final_kernel(*operands, *rest)


def final_kernel(
    rates_ref, scale_ref, taps_ref, skip_ref, incoming_ref, halo_ref, head_ref, ends_ref, gated_ref, local_ref,
    gate_ref, out_hbm, edge_ref, rows_ref, out_ref, sems,
):
    length = gated_ref.shape[0]
    mode_count = rates_ref.shape[0]
    tap_count = taps_ref.shape[1]
    halo_rows = tap_count - 1
    sublane = lax.broadcasted_iota(jnp.int32, (CHUNKS, LANES), 0)
    is_new = jnp.where(lax.axis_index("seq") == 0, 0.0, 1.0)
    copies = []
    for half in range(rates_ref.shape[1] // LANES):
        lanes = slice(half * LANES, (half + 1) * LANES)
        edges = []
        for q in range(3):
            edge_ref[q, 0:PAD, :] = halo_ref[q, :, lanes]
            edge_ref[q, PAD : 2 * PAD, :] = head_ref[q, :, lanes]
            terms = [taps_ref[q, i : i + 1, lanes] * edge_ref[q, PAD - i : 2 * PAD - i, :] for i in range(tap_count)]
            edges.append(pairwise_sum(terms))
        edge_gated = rounded(edges[1] * edges[2]) * is_new
        rates = rates_ref[:, lanes]
        scale = scale_ref[:, lanes]
        decay = jnp.exp(-rates)
        edge_state = jnp.zeros_like(decay)
        for t in range(halo_rows):
            edge_state = decay * edge_state + edge_gated[t : t + 1]
        edge_state = edge_state * jnp.exp(-rates * float(length - halo_rows))
        chunk_decay = jnp.exp(-rates * float(length))
        decays = [spread(decay[m : m + 1]) for m in range(mode_count)]
        states = []
        for m in range(mode_count):
            factor = spread(chunk_decay[m : m + 1])
            ends = ends_ref[m, :, lanes] + jnp.where(sublane == 0, spread(edge_state[m : m + 1]), 0.0)
            carried = jnp.where(sublane == 0, spread(incoming_ref[m : m + 1, lanes]), pltpu.roll(ends, 1, 0))
            for distance in (1, 2, 4):
                carried = carried + jnp.where(sublane >= distance, factor * pltpu.roll(carried, distance, 0), 0.0)
                factor = factor * factor
            states.append(carried * spread(scale[m : m + 1]))
        skip = spread(skip_ref[:, lanes])
        for j in range(length):
            states = [d * h for d, h in zip(decays, states)]
            gated, gate = gated_ref[j, :, lanes], gate_ref[j, :, lanes]
            if j < halo_rows:
                new = jnp.where(sublane == 0, spread(edge_gated[j : j + 1]), 0.0)
                states = [h + spread(scale[m : m + 1]) * new for m, h in enumerate(states)]
                gated = gated + new
                gate = jnp.where(sublane == 0, spread(edges[0][j : j + 1]), gate)
            long_out = rounded(local_ref[j, :, lanes] + pairwise_sum(states))
            rows_ref[half, pl.ds(j, CHUNKS, stride=length), :] = gate * (long_out + skip * gated)
        out_ref[half] = rows_ref[half].astype(jnp.bfloat16)
        copies.append(pltpu.make_async_copy(out_ref.at[half], out_hbm.at[:, pl.ds(half * LANES, LANES)], sems.at[half]))
        copies[-1].start()
    for copy in copies:
        copy.wait()


def shape32(*dims):
    return jax.ShapeDtypeStruct(dims, jnp.float32)


PARAMS = pltpu.CompilerParams(vmem_limit_bytes=24 * 1024 * 1024)


def on_device(projections, taps, rates, residues, skip):
    tap_count = taps.shape[0]
    halo_rows = tap_count - 1
    _, tokens, channels = projections.shape
    mode_count = rates.shape[1]
    length = tokens // CHUNKS
    halves = channels // LANES
    count = lax.axis_size("seq")
    index = lax.axis_index("seq")
    taps = taps.transpose(1, 0, 2)
    hbm = pl.BlockSpec(memory_space=pltpu.HBM)
    vmem = pl.BlockSpec(memory_space=pltpu.VMEM)
    gated, ends, state, head, tail, rates_own, scale, taps, skip = pl.pallas_call(
        state_kernel,
        out_shape=(
            shape32(length, CHUNKS, channels),
            shape32(mode_count, CHUNKS, channels),
            shape32(mode_count, channels),
            shape32(3, PAD, channels),
            shape32(3, PAD, channels),
            shape32(mode_count, channels),
            shape32(mode_count, channels),
            shape32(3, tap_count, channels),
            shape32(1, channels),
        ),
        in_specs=[hbm] * 5,
        out_specs=(vmem,) * 9,
        scratch_shapes=[
            pltpu.VMEM((halves, 2, tokens, LANES), jnp.bfloat16),
            pltpu.VMEM((2 * PAD, channels), jnp.bfloat16),
            pltpu.VMEM((2 * PAD, channels), jnp.bfloat16),
            pltpu.VMEM((mode_count, channels), jnp.float32),
            pltpu.VMEM((halves, PAD + tokens, LANES), jnp.float32),
            pltpu.VMEM((halves, PAD + tokens, LANES), jnp.float32),
            pltpu.SemaphoreType.DMA((2 * halves + 6,)),
        ],
        compiler_params=PARAMS,
        name="state",
    )(*(
        pltpu.with_memory_space_constraint(array, pltpu.HBM)
        for array in (rates.T, residues.T, taps, skip[None, :], projections)
    ))
    local, gate = pl.pallas_call(
        local_kernel,
        out_shape=(shape32(length, CHUNKS, channels),) * 2,
        in_specs=[vmem] * 5,
        out_specs=(vmem, vmem),
        scratch_shapes=[pltpu.VMEM((halves, PAD + tokens, LANES), jnp.float32)],
        compiler_params=PARAMS,
        name="local",
    )(rates_own, scale, taps, projections, gated)

    def decayed(steps):
        return jnp.exp(-rates_own * jnp.asarray(steps, jnp.float32))

    def pack(state, first, last):
        high = lax.reduce_precision(state, 8, 7)
        rows = [high, state - high, last[:, PAD - halo_rows :].reshape(3 * halo_rows, channels)]
        if first is not None:
            rows.append(first[:, :halo_rows].reshape(2 * halo_rows, channels))
        return jnp.concatenate(rows, axis=0).astype(jnp.bfloat16)

    def unpack(packed):
        packed = packed.astype(jnp.float32)
        edges = packed[2 * mode_count :].reshape(-1, halo_rows, channels)
        last = jnp.pad(edges[:3], ((0, 0), (PAD - halo_rows, 0), (0, 0)))
        first = jnp.pad(edges[3:], ((0, 0), (0, PAD - halo_rows), (0, 0)))
        return packed[:mode_count] + packed[mode_count : 2 * mode_count], first, last

    def send(packed, flip, devices):
        return lax.ppermute(packed, "seq", [(i, i ^ flip) for i in devices])

    def edge_state_of(left_last, right_first):
        joined = jnp.concatenate([left_last[1:], right_first], axis=1)
        edge = sum(taps[1:, i, None, :] * joined[:, PAD - i : 2 * PAD - i, :] for i in range(tap_count))
        gates = rounded(edge[0] * edge[1])
        edge_state = jnp.zeros_like(state)
        for t in range(halo_rows):
            edge_state = decayed(1.0) * edge_state + gates[t][None, :]
        return edge_state

    def arriving(left_state, edge_state, size):
        offset = (index % size * tokens).astype(jnp.float32)
        edge_part = decayed(jnp.maximum(offset - halo_rows, 0.0)) * edge_state
        return decayed(offset) * left_state + jnp.where(index % size == 0, 0.0, edge_part)

    def join(block, received, prefix, halo, size):
        state, first, last = block
        other_state, other_first, other_last = unpack(received)
        is_right = index // size % 2 == 1
        left_last = jnp.where(is_right, other_last, last)
        right_first = jnp.where(is_right, first, other_first)
        left_state = jnp.where(is_right, other_state, state)
        right_state = jnp.where(is_right, state, other_state)
        edge_state = edge_state_of(left_last, right_first)
        prefix = jnp.where(is_right, prefix + arriving(left_state, edge_state, size), prefix)
        halo = jnp.where(is_right & (index % size == 0), other_last, halo)
        steps = float(size * tokens)
        state = right_state + decayed(steps - halo_rows) * edge_state + decayed(steps) * left_state
        first = jnp.where(is_right, other_first, first)
        last = jnp.where(is_right, last, other_last)
        return (state, first, last), prefix, halo

    def finish(kernel, prefix, halo, *earlier):
        operands = (rates_own, scale, taps, skip, prefix, halo, head, ends, gated, local, gate)
        return pl.pallas_call(
            kernel,
            out_shape=jax.ShapeDtypeStruct((tokens, channels), jnp.bfloat16),
            in_specs=[vmem] * len(operands) + [hbm] * len(earlier),
            out_specs=hbm,
            scratch_shapes=[
                pltpu.VMEM((3, 2 * PAD, LANES), jnp.float32),
                pltpu.VMEM((halves, tokens, LANES), jnp.float32),
                pltpu.VMEM((halves, tokens, LANES), jnp.bfloat16),
                pltpu.SemaphoreType.DMA((halves,)),
            ],
            input_output_aliases={len(operands): 0} if earlier else {},
            cost_estimate=pl.CostEstimate(flops=10_000_000, bytes_accessed=2_000_000, transcendentals=0),
            compiler_params=PARAMS,
            name="final",
        )(*operands, *earlier)

    everyone, early, late = range(count), range(count // 2), range(count // 2, count)
    block, prefix, halo = (state, head[1:], tail), jnp.zeros_like(state), jnp.zeros_like(tail)
    block, prefix, halo = join(block, send(pack(*block), 1, everyone), prefix, halo, 1)
    received = send(pack(*block), 3, everyone)
    received, local, gate = lax.optimization_barrier((received, local, gate))
    block, prefix, halo = join(block, received, prefix, halo, 2)
    packed = pack(*block)
    received = lax.ppermute(packed, "seq", [(i, i ^ (5 if i in early else 1)) for i in everyone])
    joined, early_prefix, early_halo = join(block, received, prefix, halo, 4)
    out = finish(final_kernel, early_prefix, early_halo)
    total = pack(joined[0], None, joined[2])
    crossed = lax.ppermute(total, "seq", list(CROSSING.items()))
    crossed, out = lax.optimization_barrier((crossed, out))
    left_state, _, left_last = unpack(crossed)
    offset = (index % (count // 2) * tokens).astype(jnp.float32)
    is_late = index >= count // 2
    prefix = prefix + jnp.where(is_late, decayed(offset), 0.0) * left_state
    second, prefix, left_last = lax.optimization_barrier(
        (lax.ppermute(packed, "seq", [(i, i ^ (5 if i in late else 1)) for i in everyone]), prefix, left_last)
    )
    (_, first, _), prefix, halo = join(block, jnp.where(is_late, second, received), prefix, halo, 4)
    edge_part = decayed(jnp.maximum(offset - halo_rows, 0.0)) * edge_state_of(left_last, first)
    prefix = prefix + jnp.where(index > count // 2, edge_part, 0.0)
    halo = jnp.where(index == count // 2, left_last, halo)
    return finish(late_kernel, prefix, halo, out)


def solution(mesh):
    in_specs = (P(None, "seq", "fft"), P(None, None, "fft"), P(), P(), P("fft"))
    out_specs = P("seq", "fft")
    return jax.shard_map(on_device, mesh=mesh, in_specs=in_specs, out_specs=out_specs, check_vma=False)
```
